32 devices in a mesh: seq: 8 (over y, x, core), mp: 4 (over z).
Axes of the slice: x: 2, y: 2, z: 4, core: 2. Of those that a mesh axis runs over, the one named last changes fastest.
Arguments:
- qkv: bfloat16 [3, 8192, 8192], P(None, 'mp', 'seq'), may hold values from -6 to 6
- short_taps: bfloat16 [3, 8192, 7], P(None, 'mp'), may hold values from -2 to 2
- medium_taps: bfloat16 [8192, 128], P('mp'), may hold values from -0.5 to 0.5
- skip_gain: float32 [8192], P('mp'), may hold values from -4 to 4
- w_out: bfloat16 [8192, 8192], P('mp'), may hold values from -0.09375 to 0.09375
- resid: bfloat16 [8192, 8192], P('mp', 'seq'), may hold values from -6 to 6
- steer: float32 [8192], P('mp'), may hold values from -5 to 5
Outputs:
- layer_out: bfloat16 [8192, 8192], P('mp', 'seq')
The draws below stay inside these ranges and needn't reach their ends.
All inputs are finite; a program needn't handle non-finite values.
Results may differ from the reference program's by a relative error of at most 0.017.
Values may be sent and summed in bfloat16 or wider, within the bound.
A program may use at most 192 MiB of HBM per device.

```python
import jax
import jax.numpy as jnp
from jax import lax

D = 8192
STAPS = 7
MTAPS = 128
LEN = 8192
N_MP = 4


def spiked(values, own_key, source, target, parts, factor):
    def block_of(dim):
        return (jnp.arange(values.shape[dim]) // (values.shape[dim] // parts)).reshape((-1,) + (1,) * (values.ndim - 1 - dim))

    near = jax.random.permutation(own_key, parts)[block_of(target)]
    far = (block_of(target) + parts // 2) % parts
    return jnp.where((block_of(source) == near) | (block_of(source) == far), factor * values, values)


def levels(own_key, dims, cuts, low, high):
    loudness = 1.0
    for position, parts in cuts:
        heights = jax.random.uniform(jax.random.fold_in(jax.random.fold_in(own_key, 6), position), (parts,), jnp.float32, low / len(cuts), high / len(cuts))
        loudness = loudness * jnp.repeat(jnp.exp(heights), dims[position] // parts).reshape((-1,) + (1,) * (len(dims) - 1 - position))
    return loudness


def noise(own_key, extent, width, limit, pieces=(), held_as=jnp.bfloat16):
    entries = jax.random.normal(own_key, extent, jnp.float32) * width
    if len(pieces) > 0:
        entries = levels(own_key, extent, pieces, -0.22, 0.18) * entries
    return jnp.clip(entries, min=-limit, max=limit).astype(held_as)


def heavy_noise(stream_key, dims, spread, most, pieces, heavy, kind=jnp.bfloat16):
    entries = spread * jax.random.normal(stream_key, dims, jnp.float32)
    if pieces:
        entries = entries * levels(stream_key, dims, pieces, -0.22, 0.18)
    return jnp.clip(spiked(entries, jax.random.fold_in(stream_key, 3), *heavy), -most, most).astype(kind)


def setup_inputs(seed: int = 0) -> dict:
    key_list = jax.random.split(jax.random.key(seed), 8)
    return {
        "qkv": noise(key_list[0], (3, D, LEN), 1.0, 6.0, ((1, 4), (2, 8))),
        "short_taps": noise(key_list[1], (3, D, STAPS), STAPS ** -0.5, 2.0, ((1, 4),)),
        "medium_taps": noise(key_list[2], (D, MTAPS), MTAPS ** -0.5, 0.5, ((0, 4),)),
        "skip_gain": noise(key_list[3], (D,), 1.0, 4.0, ((0, 4),), jnp.float32),
        "w_out": heavy_noise(key_list[4], (D, D), D ** -0.5, 0.09375, ((0, 4),), (0, 1, 4, 2.0)),
        "resid": noise(key_list[5], (D, LEN), 1.0, 6.0, ((0, 4), (1, 8))),
        "steer": noise(key_list[6], (D,), 1.0, 5.0, ((0, 4),), jnp.float32),
    }


def short_conv(x, taps):
    length = x.shape[1]
    padded = jnp.pad(x, ((0, 0), (STAPS - 1, 0)))
    total = jnp.zeros_like(x)
    for j in range(STAPS):
        total = total + taps[:, j:j + 1] * padded[:, STAPS - 1 - j:STAPS - 1 - j + length]
    return total


def medium_block(pair):
    values, filt = pair
    length = values.shape[1]
    padded = jnp.pad(values, ((0, 0), (MTAPS - 1, 0)))

    def add_tap(j, total):
        column = lax.dynamic_slice_in_dim(filt, j, 1, 1)
        window = lax.dynamic_slice_in_dim(padded, MTAPS - 1 - j, length, 1)
        return total + column * window

    return lax.fori_loop(0, MTAPS, add_tap, jnp.zeros_like(values))


def reference(qkv, short_taps, medium_taps, skip_gain, w_out, resid, steer):
    f32 = jnp.float32
    taps = short_taps.astype(f32)
    q_filt = short_conv(qkv[0].astype(f32), taps[0])
    k_filt = short_conv(qkv[1].astype(f32), taps[1])
    v_filt = short_conv(qkv[2].astype(f32), taps[2])
    kv = (k_filt * v_filt).astype(jnp.bfloat16)
    kv_wide = kv.astype(f32)
    block = min(D, 256)
    length = kv.shape[1]
    blocks = lax.map(medium_block, (kv_wide.reshape(D // block, block, length), medium_taps.astype(f32).reshape(D // block, block, MTAPS)))
    med = blocks.reshape(D, length) + skip_gain.astype(f32)[:, None] * kv_wide
    y_out = (q_filt * med).astype(jnp.bfloat16)
    group = D // N_MP

    def add_group(g, total):
        y_part = lax.dynamic_slice_in_dim(y_out, g * group, group, 0).astype(f32)
        w_part = lax.dynamic_slice_in_dim(w_out, g * group, group, 0).astype(f32)
        part = jnp.dot(w_part.T, y_part, precision=lax.Precision.HIGHEST)
        rounded = lax.optimization_barrier(part.astype(jnp.bfloat16))
        return total + rounded.astype(f32)

    proj = lax.fori_loop(0, N_MP, add_group, jnp.zeros((D, length), f32))
    return (resid.astype(f32) + proj + steer.astype(f32)[:, None]).astype(jnp.bfloat16)
```

```python
import jax
import jax.numpy as jnp
from jax import lax
from jax.experimental import pallas as pl
from jax.experimental.pallas import tpu as pltpu
from jax.sharding import PartitionSpec as P

STAPS = 7
MTAPS = 128
WINDOW = 256
LANES = 128
F32 = jnp.float32
BF16 = jnp.bfloat16


def from_behind(value, axis, steps):
    count = lax.axis_size(axis)
    return lax.ppermute(value, axis, [(source, source + steps) for source in range(count - steps)])


def feature_kernel(before_ref, now_ref, short_ref, medium_ref, y_ref, wide, kv):
    for s in range(3):
        wide[s, :WINDOW] = before_ref[s].astype(F32).T
        wide[s, WINDOW:] = now_ref[s].astype(F32).T

    def short(s, row):
        total = short_ref[s, 0:1] * wide[s, row : row + LANES]
        for j in range(1, STAPS):
            total = total + short_ref[s, j : j + 1] * wide[s, row - j : row - j + LANES]
        return total

    for row in range(WINDOW - MTAPS, 2 * WINDOW, LANES):
        place = row - (WINDOW - MTAPS)
        kv[place : place + LANES] = (short(1, row) * short(2, row)).astype(BF16).astype(F32)

    for row in range(0, WINDOW, LANES):
        total = jnp.zeros((LANES, LANES), F32)
        for low in range(8):
            start = row + 8 - low
            block = kv[start : start + LANES + MTAPS - 8]
            for high in range(0, MTAPS, 8):
                first = MTAPS - 8 - high
                total = total + medium_ref[high + low : high + low + 1] * block[first : first + LANES]
        y_ref[:, row : row + LANES] = (short(0, WINDOW + row) * total).T.astype(BF16)


def features(before, before_index, now, now_index, short, medium):
    channels = now.shape[1]
    return pl.pallas_call(
        feature_kernel,
        grid=(channels // LANES,),
        in_specs=[
            pl.BlockSpec((3, LANES, WINDOW), lambda c: (0, c, before_index)),
            pl.BlockSpec((3, LANES, WINDOW), lambda c: (0, c, now_index)),
            pl.BlockSpec((3, STAPS, LANES), lambda c: (0, 0, c)),
            pl.BlockSpec((MTAPS, LANES), lambda c: (0, c)),
        ],
        out_specs=pl.BlockSpec((LANES, WINDOW), lambda c: (c, 0)),
        out_shape=jax.ShapeDtypeStruct((channels, WINDOW), BF16),
        scratch_shapes=[
            pltpu.VMEM((3, 2 * WINDOW, LANES), F32),
            pltpu.VMEM((MTAPS + WINDOW, LANES), F32),
        ],
        cost_estimate=pl.CostEstimate(
            flops=2 * channels * WINDOW * (MTAPS + 4 * STAPS),
            bytes_accessed=14 * channels * WINDOW,
            transcendentals=0,
        ),
    )(before, now, short, medium)


def shards(qkv, short_taps, medium_taps, skip_gain, w_out, resid, steer):
    slab = qkv.shape[2]
    short = jnp.swapaxes(short_taps.astype(F32), 1, 2)
    medium = medium_taps.astype(F32)
    medium = jnp.concatenate([medium[:, :1] + skip_gain[:, None], medium[:, 1:]], 1).T
    rim = from_behind(qkv[:, :, slab - WINDOW :], "seq", 1)
    count = slab // WINDOW
    pieces = [None] * count
    for i in reversed(range(count)):
        before = (rim, 0) if i == 0 else (qkv, i - 1)
        y = features(*before, qkv, i, short, medium)
        part = lax.dot_general(
            w_out, y, (((0,), (0,)), ((), ())), preferred_element_type=F32
        ).astype(BF16)
        proj = lax.psum_scatter(part, "mp", scatter_dimension=0, tiled=True).astype(F32)
        own = resid[:, i * WINDOW : (i + 1) * WINDOW].astype(F32)
        pieces[i] = (own + proj + steer[:, None]).astype(BF16)
    return jnp.concatenate(pieces, 1)


def solution(mesh):
    return jax.shard_map(
        shards,
        mesh=mesh,
        in_specs=(
            P(None, "mp", "seq"),
            P(None, "mp", None),
            P("mp", None),
            P("mp"),
            P("mp", None),
            P("mp", "seq"),
            P("mp"),
        ),
        out_specs=P("mp", "seq"),
        check_vma=False,
    )
```

```python
import functools

import jax
import jax.numpy as jnp
from jax import lax
from jax.experimental import pallas as pl
from jax.experimental.pallas import tpu as pltpu
from jax.sharding import PartitionSpec as P

STAPS = 7
MTAPS = 128
LANES = 128
F32 = jnp.float32
BF16 = jnp.bfloat16


def from_behind(value, axis, steps):
    count = lax.axis_size(axis)
    return lax.ppermute(value, axis, [(source, source + steps) for source in range(count - steps)])


def chunks(slab):
    plan = [(slab - LANES, LANES, False), (slab - 2 * LANES, LANES, False)]
    for first in range(slab - 4 * LANES, -1, -2 * LANES):
        plan.append((first, 2 * LANES, False))
    return plan


def feature_kernel(blocks, *refs):
    token_refs = refs[:blocks]
    short_ref, medium_ref, y_ref, wide, kv = refs[blocks:]
    for at, ref in enumerate(token_refs):
        for s in range(3):
            if s > 0 or at > 0:
                wide[s, at * LANES : (at + 1) * LANES] = ref[s].astype(F32).T

    def short(s, row):
        total = short_ref[s, 0:1] * wide[s, row : row + LANES]
        for j in range(1, STAPS):
            total = total + short_ref[s, j : j + 1] * wide[s, row - j : row - j + LANES]
        return total

    for at in range(1, blocks):
        row = at * LANES
        kv[row - LANES : row] = (short(1, row) * short(2, row)).astype(BF16).astype(F32)

    for at in range(blocks - 2):
        row = at * LANES
        total = jnp.zeros((LANES, LANES), F32)
        for low in range(8):
            start = row + 8 - low
            block = kv[start : start + LANES + MTAPS - 8]
            for high in range(0, MTAPS, 8):
                first = MTAPS - 8 - high
                total = total + medium_ref[high + low : high + low + 1] * block[first : first + LANES]
        y_ref[row : row + LANES] = (short(0, row + 2 * LANES) * total).astype(BF16)


def features(sources, short, medium):
    channels = short.shape[2]
    blocks = len(sources)
    tokens = (blocks - 2) * LANES
    return pl.pallas_call(
        functools.partial(feature_kernel, blocks),
        grid=(channels // LANES,),
        in_specs=[pl.BlockSpec((3, LANES, LANES), lambda c, at=at: (0, c, at)) for _, at in sources]
        + [
            pl.BlockSpec((3, STAPS, LANES), lambda c: (0, 0, c)),
            pl.BlockSpec((MTAPS, LANES), lambda c: (0, c)),
        ],
        out_specs=pl.BlockSpec((tokens, LANES), lambda c: (0, c)),
        out_shape=jax.ShapeDtypeStruct((tokens, channels), BF16),
        scratch_shapes=[
            pltpu.VMEM((3, blocks * LANES, LANES), F32),
            pltpu.VMEM(((blocks - 1) * LANES, LANES), F32),
        ],
        cost_estimate=pl.CostEstimate(
            flops=2 * channels * tokens * (MTAPS + 4 * STAPS),
            bytes_accessed=6 * channels * blocks * LANES,
            transcendentals=0,
        ),
    )(*[array for array, _ in sources], short, medium)


def finish_kernel(*refs):
    resid_ref, steer_ref, proj_ref, out_ref = refs[0], refs[1], refs[2], refs[-1]
    gain = proj_ref[...].astype(F32) + steer_ref[...]
    out_ref[...] = (resid_ref[...].astype(F32) + gain.T).astype(BF16)


def finish(resid, steer, proj, out, first):
    tokens, channels = proj.shape
    rows = min(channels, 512)
    at = first // tokens
    column = pl.BlockSpec((rows, tokens), lambda c: (c, at))
    specs = [
        column,
        pl.BlockSpec((1, rows), lambda c: (0, c)),
        pl.BlockSpec((tokens, rows), lambda c: (0, c)),
    ]
    held = [] if out is None else [out]
    return pl.pallas_call(
        finish_kernel,
        grid=(channels // rows,),
        in_specs=specs + [pl.BlockSpec(memory_space=pl.ANY)] * len(held),
        out_specs=column,
        out_shape=jax.ShapeDtypeStruct(resid.shape, BF16),
        input_output_aliases={3: 0} if held else {},
        cost_estimate=pl.CostEstimate(
            flops=2 * channels * tokens, bytes_accessed=6 * channels * tokens, transcendentals=0
        ),
    )(resid, steer, proj, *held)


def relay(part, axis):
    count = lax.axis_size(axis)
    me = lax.axis_index(axis)
    width = part.shape[1] // count

    def block(owner):
        return lax.dynamic_slice_in_dim(part, jnp.clip(owner, 0, count - 1) * width, width, 1)

    own = block(me).astype(F32)
    for way in (1, -1):
        total = None
        for step in range(count - 1):
            term = block(me + way * (count - 1 - step))
            if total is not None:
                term = (term.astype(F32) + total.astype(F32)).astype(BF16)
            pairs = [(z, z + 1) for z in range(step + 1)]
            if way < 0:
                pairs = [(count - 1 - a, count - 1 - b) for a, b in pairs]
            total = lax.ppermute(term, axis, pairs)
        own = own + total.astype(F32)
    return own.astype(BF16)


def shards(qkv, short_taps, medium_taps, skip_gain, w_out, resid, steer):
    slab = qkv.shape[2]
    short = jnp.swapaxes(short_taps.astype(F32), 1, 2)
    medium = medium_taps.astype(F32)
    medium = jnp.concatenate([medium[:, :1] + skip_gain[:, None], medium[:, 1:]], 1).T
    rim = from_behind(qkv[:, :, slab - 2 * LANES :], "seq", 1)
    out = None
    projs = []
    for first, tokens, by_relay in chunks(slab):
        at = first // LANES
        sources = [(rim, i + 2) if i < 0 else (qkv, i) for i in range(at - 2, at + tokens // LANES)]
        y = features(sources, short, medium)
        part = jnp.dot(y, w_out, preferred_element_type=F32).astype(BF16)
        if by_relay:
            proj = relay(part, "mp")
        else:
            proj = lax.psum_scatter(part, "mp", scatter_dimension=1, tiled=True)
        projs.append((first, proj))
    for first, proj in projs:
        out = finish(resid, steer[None], proj, out, first)
    return out


def solution(mesh):
    return jax.shard_map(
        shards,
        mesh=mesh,
        in_specs=(
            P(None, "mp", "seq"),
            P(None, "mp", None),
            P("mp", None),
            P("mp"),
            P("mp", None),
            P("mp", "seq"),
            P("mp"),
        ),
        out_specs=P("mp", "seq"),
        check_vma=False,
    )
```

```python
import functools

import jax
import jax.numpy as jnp
from jax import lax
from jax.experimental import pallas as pl
from jax.experimental.pallas import tpu as pltpu
from jax.sharding import PartitionSpec as P

STAPS = 7
MTAPS = 128
LANES = 128
F32 = jnp.float32
BF16 = jnp.bfloat16


def from_behind(value, axis, steps):
    count = lax.axis_size(axis)
    return lax.ppermute(value, axis, [(source, source + steps) for source in range(count - steps)])


def chunks(slab):
    plan = [(slab - LANES, LANES, False)]
    for first in range(slab - 3 * LANES, 0, -2 * LANES):
        plan.append((first, 2 * LANES, first == LANES))
    return plan + [(0, LANES, False)]


def feature_kernel(blocks, *refs):
    token_refs = refs[:blocks]
    short_ref, medium_ref, y_ref, wide, kv = refs[blocks:]
    for at, ref in enumerate(token_refs):
        for s in range(3):
            if s > 0 or at > 0:
                wide[s, at * LANES : (at + 1) * LANES] = ref[s].astype(F32).T

    def short(s, row):
        total = short_ref[s, 0:1] * wide[s, row : row + LANES]
        for j in range(1, STAPS):
            total = total + short_ref[s, j : j + 1] * wide[s, row - j : row - j + LANES]
        return total

    for at in range(1, blocks):
        row = at * LANES
        kv[row - LANES : row] = (short(1, row) * short(2, row)).astype(BF16).astype(F32)

    for at in range(blocks - 2):
        row = at * LANES
        total = jnp.zeros((LANES, LANES), F32)
        for low in range(8):
            start = row + 8 - low
            block = kv[start : start + LANES + MTAPS - 8]
            for high in range(0, MTAPS, 8):
                first = MTAPS - 8 - high
                total = total + medium_ref[high + low : high + low + 1] * block[first : first + LANES]
        y_ref[row : row + LANES] = (short(0, row + 2 * LANES) * total).astype(BF16)


def features(sources, short, medium):
    channels = short.shape[2]
    blocks = len(sources)
    tokens = (blocks - 2) * LANES
    return pl.pallas_call(
        functools.partial(feature_kernel, blocks),
        grid=(channels // LANES,),
        in_specs=[pl.BlockSpec((3, LANES, LANES), lambda c, at=at: (0, c, at)) for _, at in sources]
        + [
            pl.BlockSpec((3, STAPS, LANES), lambda c: (0, 0, c)),
            pl.BlockSpec((MTAPS, LANES), lambda c: (0, c)),
        ],
        out_specs=pl.BlockSpec((tokens, LANES), lambda c: (0, c)),
        out_shape=jax.ShapeDtypeStruct((tokens, channels), BF16),
        scratch_shapes=[
            pltpu.VMEM((3, blocks * LANES, LANES), F32),
            pltpu.VMEM(((blocks - 1) * LANES, LANES), F32),
        ],
        cost_estimate=pl.CostEstimate(
            flops=2 * channels * tokens * (MTAPS + 4 * STAPS),
            bytes_accessed=6 * channels * blocks * LANES,
            transcendentals=0,
        ),
    )(*[array for array, _ in sources], short, medium)


def finish_kernel(*refs):
    resid_ref, steer_ref, proj_ref, out_ref = refs[0], refs[1], refs[2], refs[-1]
    gain = proj_ref[...].astype(F32) + steer_ref[...]
    out_ref[...] = (resid_ref[...].astype(F32) + gain.T).astype(BF16)


def finish(resid, steer, proj, out, first):
    tokens, channels = proj.shape
    rows = min(channels, 1024)
    at = first // LANES
    column = pl.BlockSpec((rows, LANES), lambda t, c: (c, at + t))
    specs = [
        column,
        pl.BlockSpec((1, rows), lambda t, c: (0, c)),
        pl.BlockSpec((LANES, rows), lambda t, c: (t, c)),
    ]
    held = [] if out is None else [out]
    return pl.pallas_call(
        finish_kernel,
        grid=(tokens // LANES, channels // rows),
        in_specs=specs + [pl.BlockSpec(memory_space=pl.ANY)] * len(held),
        out_specs=column,
        out_shape=jax.ShapeDtypeStruct(resid.shape, BF16),
        input_output_aliases={3: 0} if held else {},
        cost_estimate=pl.CostEstimate(
            flops=2 * channels * tokens, bytes_accessed=6 * channels * tokens, transcendentals=0
        ),
    )(resid, steer, proj, *held)


def relay(part, axis):
    count = lax.axis_size(axis)
    me = lax.axis_index(axis)
    width = part.shape[1] // count

    def block(owner):
        return lax.dynamic_slice_in_dim(part, jnp.clip(owner, 0, count - 1) * width, width, 1)

    own = block(me).astype(F32)
    for way in (1, -1):
        total = None
        for step in range(count - 1):
            term = block(me + way * (count - 1 - step))
            if total is not None:
                term = (term.astype(F32) + total.astype(F32)).astype(BF16)
            pairs = [(z, z + 1) for z in range(step + 1)]
            if way < 0:
                pairs = [(count - 1 - a, count - 1 - b) for a, b in pairs]
            total = lax.ppermute(term, axis, pairs)
        own = own + total.astype(F32)
    return own.astype(BF16)


def shards(qkv, short_taps, medium_taps, skip_gain, w_out, resid, steer):
    slab = qkv.shape[2]
    short = jnp.swapaxes(short_taps.astype(F32), 1, 2)
    medium = medium_taps.astype(F32)
    medium = jnp.concatenate([medium[:, :1] + skip_gain[:, None], medium[:, 1:]], 1).T
    rim = from_behind(qkv[:, :, slab - 2 * LANES :], "seq", 1)
    out = None
    projs = []
    for first, tokens, by_relay in chunks(slab):
        at = first // LANES
        sources = [(rim, i + 2) if i < 0 else (qkv, i) for i in range(at - 2, at + tokens // LANES)]
        y = features(sources, short, medium)
        part = jnp.dot(y, w_out, preferred_element_type=F32).astype(BF16)
        if by_relay:
            proj = relay(part, "mp")
        else:
            proj = lax.psum_scatter(part, "mp", scatter_dimension=1, tiled=True)
        projs.append((first, proj))
    for first, proj in projs:
        out = finish(resid, steer[None], proj, out, first)
    return out


def solution(mesh):
    return jax.shard_map(
        shards,
        mesh=mesh,
        in_specs=(
            P(None, "mp", "seq"),
            P(None, "mp", None),
            P("mp", None),
            P("mp"),
            P("mp", None),
            P("mp", "seq"),
            P("mp"),
        ),
        out_specs=P("mp", "seq"),
        check_vma=False,
    )
```

```python
import functools

import jax
import jax.numpy as jnp
from jax import lax
from jax.experimental import pallas as pl
from jax.experimental.pallas import tpu as pltpu
from jax.sharding import PartitionSpec as P

STAPS = 7
MTAPS = 128
LANES = 128
F32 = jnp.float32
BF16 = jnp.bfloat16


def from_behind(value, axis, steps):
    count = lax.axis_size(axis)
    return lax.ppermute(value, axis, [(source, source + steps) for source in range(count - steps)])


def chunks(slab):
    sizes = [1]
    left = slab // LANES - 3
    while left > 0:
        sizes.append(min(left, 2 if len(sizes) == 1 else 3))
        left -= sizes[-1]
    sizes.append(2)
    plan, end = [], slab
    for size in sizes:
        end -= size * LANES
        plan.append((end, size * LANES))
    return plan


def feature_kernel(blocks, *refs):
    token_refs = refs[:blocks]
    short_ref, medium_ref, y_ref, wide, kv = refs[blocks:]
    for at, ref in enumerate(token_refs):
        for s in range(3):
            if s > 0 or at > 0:
                wide[s, at * LANES : (at + 1) * LANES] = ref[s].astype(F32).T

    def short(s, row):
        total = short_ref[s, 0:1] * wide[s, row : row + LANES]
        for j in range(1, STAPS):
            total = total + short_ref[s, j : j + 1] * wide[s, row - j : row - j + LANES]
        return total

    for at in range(1, blocks):
        row = at * LANES
        kv[row - LANES : row] = (short(1, row) * short(2, row)).astype(BF16).astype(F32)

    for at in range(blocks - 2):
        row = at * LANES
        total = jnp.zeros((LANES, LANES), F32)
        for low in range(8):
            start = row + 8 - low
            block = kv[start : start + LANES + MTAPS - 8]
            for high in range(0, MTAPS, 8):
                first = MTAPS - 8 - high
                total = total + medium_ref[high + low : high + low + 1] * block[first : first + LANES]
        y_ref[row : row + LANES] = (short(0, row + 2 * LANES) * total).astype(BF16)


def features(sources, short, medium):
    channels = short.shape[2]
    blocks = len(sources)
    tokens = (blocks - 2) * LANES
    return pl.pallas_call(
        functools.partial(feature_kernel, blocks),
        grid=(channels // LANES,),
        in_specs=[pl.BlockSpec((3, LANES, LANES), lambda c, at=at: (0, c, at)) for _, at in sources]
        + [
            pl.BlockSpec((3, STAPS, LANES), lambda c: (0, 0, c)),
            pl.BlockSpec((MTAPS, LANES), lambda c: (0, c)),
        ],
        out_specs=pl.BlockSpec((tokens, LANES), lambda c: (0, c)),
        out_shape=jax.ShapeDtypeStruct((tokens, channels), BF16),
        scratch_shapes=[
            pltpu.VMEM((3, blocks * LANES, LANES), F32),
            pltpu.VMEM(((blocks - 1) * LANES, LANES), F32),
        ],
        cost_estimate=pl.CostEstimate(
            flops=2 * channels * tokens * (MTAPS + 4 * STAPS),
            bytes_accessed=6 * channels * blocks * LANES,
            transcendentals=0,
        ),
    )(*[array for array, _ in sources], short, medium)


def finish_kernel(*refs):
    resid_ref, steer_ref, proj_ref, out_ref = refs[0], refs[1], refs[2], refs[-1]
    gain = proj_ref[...].astype(F32) + steer_ref[...]
    out_ref[...] = (resid_ref[...].astype(F32) + gain.T).astype(BF16)


def finish(resid, steer, proj, out, first):
    tokens, channels = proj.shape
    rows = min(channels, 1024)
    at = first // LANES
    column = pl.BlockSpec((rows, LANES), lambda t, c: (c, at + t))
    specs = [
        column,
        pl.BlockSpec((1, rows), lambda t, c: (0, c)),
        pl.BlockSpec((LANES, rows), lambda t, c: (t, c)),
    ]
    held = [] if out is None else [out]
    return pl.pallas_call(
        finish_kernel,
        grid=(tokens // LANES, channels // rows),
        in_specs=specs + [pl.BlockSpec(memory_space=pl.ANY)] * len(held),
        out_specs=column,
        out_shape=jax.ShapeDtypeStruct(resid.shape, BF16),
        input_output_aliases={3: 0} if held else {},
        cost_estimate=pl.CostEstimate(
            flops=2 * channels * tokens, bytes_accessed=6 * channels * tokens, transcendentals=0
        ),
    )(resid, steer, proj, *held)


def shards(qkv, short_taps, medium_taps, skip_gain, w_out, resid, steer):
    slab = qkv.shape[2]
    short = jnp.swapaxes(short_taps.astype(F32), 1, 2)
    medium = medium_taps.astype(F32)
    medium = jnp.concatenate([medium[:, :1] + skip_gain[:, None], medium[:, 1:]], 1).T
    rim = from_behind(qkv[:, :, slab - 2 * LANES :], "seq", 1)
    out = None
    projs = []
    for first, tokens in chunks(slab):
        at = first // LANES
        sources = [(rim, i + 2) if i < 0 else (qkv, i) for i in range(at - 2, at + tokens // LANES)]
        y = features(sources, short, medium)
        part = jnp.dot(y, w_out, preferred_element_type=F32).astype(BF16)
        proj = lax.psum_scatter(part, "mp", scatter_dimension=1, tiled=True)
        projs.append((first, proj))
    for first, proj in projs:
        out = finish(resid, steer[None], proj, out, first)
    return out


def solution(mesh):
    return jax.shard_map(
        shards,
        mesh=mesh,
        in_specs=(
            P(None, "mp", "seq"),
            P(None, "mp", None),
            P("mp", None),
            P("mp"),
            P("mp", None),
            P("mp", "seq"),
            P("mp"),
        ),
        out_specs=P("mp", "seq"),
        check_vma=False,
    )
```
